32 devices in a mesh: groups: 2 (over x), dp: 8 (over z, y), ctx: 2 (over core).
Axes of the slice: x: 2, y: 2, z: 4, core: 2. Of those that a mesh axis runs over, the one named last changes fastest.
Arguments:
- queries: bfloat16 [16, 768, 2048], P(('groups', 'dp'), 'ctx'), parts along dimension 0, may hold values from -8 to 8
- keys: bfloat16 [16, 768, 512], P(('groups', 'dp'), 'ctx'), parts along dimension 0, may hold values from -8 to 8
- values: bfloat16 [16, 768, 512], P(('groups', 'dp'), 'ctx'), parts along dimension 0, may hold values from -6 to 6
- out_grad: bfloat16 [16, 768, 2048], P(('groups', 'dp'), 'ctx'), parts along dimension 0, may hold values from -6 to 6
- key_weight: bfloat16 [4096, 512], P('ctx'), may hold values from -0.09375 to 0.09375
- value_weight: bfloat16 [4096, 512], P('ctx'), may hold values from -0.09375 to 0.09375
- suffix_embed: bfloat16 [32, 8, 4096], P(('groups', 'dp'), None, 'ctx'), parts along dimension 0, may hold values from -6 to 6
- class_ids: int32 [16], P(('groups', 'dp')), parts along dimension 0, may hold values from 0 to 15
- class_slot: int32 [32], P('groups'), parts along dimension 0, may hold values from 0 to 15, each once
- pad_offset: int32 [16], P(('groups', 'dp')), parts along dimension 0, may hold values from 0 to 384, as said below
- suffix_pos: int32 [16, 8], P(('groups', 'dp')), parts along dimension 0, may hold values from 0 to 767, as said below
Outputs:
- query_grad: bfloat16 [16, 768, 2048], P(('groups', 'dp'), 'ctx'), parts along dimension 0
- key_grad: bfloat16 [16, 768, 512], P(('groups', 'dp'), 'ctx'), parts along dimension 0
- value_grad: bfloat16 [16, 768, 512], P(('groups', 'dp'), 'ctx'), parts along dimension 0
- suffix_grad: float32 [32, 8, 4096], P(('groups', 'dp'), None, 'ctx'), parts along dimension 0
The draws below stay inside these ranges and needn't reach their ends.
There are 2 independent parts, one for each index of `groups`. The reference program is written for one: setup_inputs(seed, part) draws one part's arguments, and reference() takes and returns one part's arrays. A program takes and returns all parts, laid end to end along the dimension named above; an argument that names none is the same for every part. Nothing has to cross between parts.
Inputs may be any that keep to these rules, and one draw needn't show every extreme that they name: `class_slot`: each class gets a distinct slot. `pad_offset`: reached by some prompt. `suffix_pos`: every suffix position of a prompt is at least its pad_offset; the smallest and the largest are reached.
All inputs are finite; a program needn't handle non-finite values.
Results may differ from the reference program's by a relative error of at most 0.039.
Values may be sent and summed in bfloat16 or wider, within the bound.
A program may use at most 128 MiB of HBM per device.

```python
import jax
import jax.numpy as jnp
from jax import lax

D = 4096
HEADS = 16
KV_HEADS = 4
HEAD_DIM = 128
SUFFIX = 8
GROUP = 4
LENGTH = 768
SAMPLES = 8
CLASSES = 16


def draw_queries(key, part):
    base = jnp.clip(jax.random.normal(jax.random.fold_in(key, 1), (SAMPLES, LENGTH, HEADS * HEAD_DIM), jnp.float32), -6.0, 6.0)
    return base.astype(jnp.bfloat16)


def draw_keys(key, part):
    base = jnp.clip(jax.random.normal(jax.random.fold_in(key, 2), (SAMPLES, LENGTH, KV_HEADS * HEAD_DIM), jnp.float32), -6.0, 6.0)
    return base.astype(jnp.bfloat16)


def offsets_of(key):
    raw_offset = jax.random.randint(jax.random.fold_in(key, 21), (SAMPLES,), 0, LENGTH // 2 + 1)
    chosen = jax.random.randint(jax.random.fold_in(key, 23), (), 0, SAMPLES)
    raw_offset = raw_offset.at[chosen].set(LENGTH // 2)
    return raw_offset.at[(chosen + 1) % SAMPLES].set(0).astype(jnp.int32)


def draw_pad_offset(key, part):
    return offsets_of(key)


def draw_suffix_pos(key, part):
    offsets = offsets_of(key)
    span_left = LENGTH - offsets
    raw_pos = jax.random.randint(jax.random.fold_in(key, 22), (SAMPLES, SUFFIX), 0, LENGTH)
    placed = offsets[:, None] + raw_pos % span_left[:, None]
    chosen = jax.random.randint(jax.random.fold_in(key, 24), (), 0, SAMPLES)
    placed = placed.at[chosen, 0].set(LENGTH - 1)
    unpadded = jnp.argmin(offsets)
    placed = placed.at[unpadded, SUFFIX - 1].set(0)
    return placed.astype(jnp.int32)


def place_ends(result, stream_key, low, largest):
    extent = result.shape
    spot = [jax.random.randint(jax.random.fold_in(stream_key, axis), (), 0, extent[axis]) for axis in range(len(extent))]
    result = result.at[tuple(spot)].set(low)
    longest = extent.index(max(extent))
    spot[longest] = (spot[longest] + 1) % extent[longest]
    return result.at[tuple(spot)].set(largest)


def block_scale(stream_key, shape, shards, low, top_value):
    def one(axis_at, parts):
        draws = jax.random.uniform(jax.random.fold_in(jax.random.fold_in(stream_key, 6), axis_at), (parts,), jnp.float32, low / len(shards), top_value / len(shards))
        return jnp.repeat(jnp.exp(draws), shape[axis_at] // parts).reshape((-1,) + (1,) * (len(shape) - axis_at - 1))

    loudness = one(*shards[0])
    for cut in shards[1:]:
        loudness = loudness * one(*cut)
    return loudness


def normal_values(key, extent, width, bound, pieces=(), kind=jnp.bfloat16):
    level = block_scale(key, extent, pieces, -0.22, 0.18) if pieces else 1.0
    values = jax.random.normal(key, extent, jnp.float32) * width * level
    return jnp.minimum(jnp.maximum(values, -bound), bound).astype(kind)


def setup_inputs(seed: int = 0, part: int = 0) -> dict:
    splits = jax.random.split(jax.random.key(seed), 12)
    own_keys = jax.random.split(jax.random.fold_in(splits[11], part), 12)
    queries = draw_queries(jax.random.fold_in(jax.random.fold_in(splits[11], part), 71), part)
    keys = draw_keys(jax.random.fold_in(jax.random.fold_in(splits[11], part), 71), part)
    values = normal_values(own_keys[2], (SAMPLES, LENGTH, KV_HEADS * HEAD_DIM), 1.0, 6.0, ((0, 8), (1, 2)))
    out_grad = normal_values(own_keys[3], (SAMPLES, LENGTH, HEADS * HEAD_DIM), 1.0, 6.0, ((0, 8), (1, 2)))
    key_weight = normal_values(splits[4], (D, KV_HEADS * HEAD_DIM), D ** -0.5, 0.09375, ((0, 2),))
    value_weight = normal_values(splits[5], (D, KV_HEADS * HEAD_DIM), D ** -0.5, 0.09375, ((0, 2),))
    suffix_embed = normal_values(own_keys[6], (CLASSES, SUFFIX, D), 1.0, 6.0, ((0, 8), (2, 2)))
    class_ids = place_ends(jax.random.randint(own_keys[7], (SAMPLES,), 0, CLASSES), jax.random.fold_in(own_keys[7], 1), 0, CLASSES - 1).astype(jnp.int32)
    class_slot = jax.random.permutation(own_keys[8], CLASSES).astype(jnp.int32)
    pad_offset = draw_pad_offset(jax.random.fold_in(jax.random.fold_in(splits[11], part), 71), part)
    suffix_pos = draw_suffix_pos(jax.random.fold_in(jax.random.fold_in(splits[11], part), 71), part)
    return {"queries": queries, "keys": keys, "values": values, "out_grad": out_grad, "key_weight": key_weight, "value_weight": value_weight, "suffix_embed": suffix_embed, "class_ids": class_ids, "class_slot": class_slot, "pad_offset": pad_offset, "suffix_pos": suffix_pos}


masked_fill = -1.0e30


def round_half(value):
    return lax.optimization_barrier(value.astype(jnp.bfloat16)).astype(jnp.float32)


def attend_one(operands):
    queries_one, kv_one, grads_one, suffix_one, offset, positions = operands
    scale = HEAD_DIM ** -0.5
    kv_width = KV_HEADS * HEAD_DIM
    token_pos = jnp.arange(LENGTH, dtype=jnp.int32)
    earlier = token_pos[None, :] <= token_pos[:, None]
    kept = (token_pos[None, :] >= offset) | (token_pos[None, :] == token_pos[:, None])
    suffix_seen = positions[None, :] <= token_pos[:, None]
    visible = jnp.concatenate([earlier & kept, suffix_seen], axis=1)
    every_kv = jnp.concatenate([kv_one, suffix_one], axis=0).astype(jnp.float32)
    dq_list = []
    dk_list = []
    dv_list = []
    for kv_head in range(KV_HEADS):
        low = kv_head * GROUP * HEAD_DIM
        high = (kv_head + 1) * GROUP * HEAD_DIM
        query_part = queries_one[:, low:high].reshape(LENGTH, GROUP, HEAD_DIM).astype(jnp.float32)
        grad_part = grads_one[:, low:high].reshape(LENGTH, GROUP, HEAD_DIM).astype(jnp.float32)
        keys_part = every_kv[:, kv_head * HEAD_DIM:(kv_head + 1) * HEAD_DIM]
        values_part = every_kv[:, kv_width + kv_head * HEAD_DIM:kv_width + (kv_head + 1) * HEAD_DIM]
        scores = jnp.einsum("pgd,jd->gpj", query_part, keys_part, precision=lax.Precision.HIGHEST) * scale
        scores = jnp.where(visible[None], scores, masked_fill)
        row_max = jnp.max(scores, axis=2)
        expo = jnp.exp(scores - row_max[:, :, None])
        total = jnp.sum(expo, axis=2)
        mixed = jnp.einsum("gpj,jd->pgd", round_half(expo), values_part, precision=lax.Precision.HIGHEST)
        attended = round_half(mixed / total.T[:, :, None])
        delta = jnp.sum(grad_part * attended, axis=2).T
        probs = expo / total[:, :, None]
        prob_grad = jnp.einsum("pgd,jd->gpj", grad_part, values_part, precision=lax.Precision.HIGHEST)
        score_grad = round_half(probs * (prob_grad - delta[:, :, None]))
        query_piece = jnp.einsum("gpj,jd->pgd", score_grad, keys_part, precision=lax.Precision.HIGHEST)
        dq_list.append(query_piece.reshape(LENGTH, GROUP * HEAD_DIM) * scale)
        dk_list.append(jnp.einsum("gpj,pgd->jd", score_grad, query_part, precision=lax.Precision.HIGHEST) * scale)
        dv_list.append(jnp.einsum("gpj,pgd->jd", round_half(probs), grad_part, precision=lax.Precision.HIGHEST))
    query_grad = jnp.concatenate(dq_list, axis=1).astype(jnp.bfloat16)
    every_grad = jnp.concatenate(dk_list + dv_list, axis=1)
    return query_grad, every_grad[:LENGTH], every_grad[LENGTH:]


def reference(queries, keys, values, out_grad, key_weight, value_weight, suffix_embed, class_ids, class_slot, pad_offset, suffix_pos):
    kv_width = KV_HEADS * HEAD_DIM
    slots = class_slot[class_ids]
    chosen = suffix_embed[slots].astype(jnp.float32)
    key_full = key_weight.astype(jnp.float32)
    value_full = value_weight.astype(jnp.float32)
    suffix_keys = jnp.einsum("bsd,dk->bsk", chosen, key_full, precision=lax.Precision.HIGHEST)
    suffix_values = jnp.einsum("bsd,dk->bsk", chosen, value_full, precision=lax.Precision.HIGHEST)
    suffix_kv = jnp.concatenate([suffix_keys, suffix_values], axis=2).astype(jnp.bfloat16)
    every_kv = jnp.concatenate([keys, values], axis=2)
    query_grad, prompt_grad, suffix_grads = lax.map(attend_one, (queries, every_kv, out_grad, suffix_kv, pad_offset, suffix_pos))
    contrib = jnp.einsum("bsk,dk->bsd", suffix_grads[:, :, :kv_width], key_full, precision=lax.Precision.HIGHEST)
    contrib = contrib + jnp.einsum("bsk,dk->bsd", suffix_grads[:, :, kv_width:], value_full, precision=lax.Precision.HIGHEST)
    suffix_grad = jnp.zeros((CLASSES, SUFFIX, D), jnp.float32).at[slots].add(contrib)
    key_grad = prompt_grad[:, :, :kv_width].astype(jnp.bfloat16)
    value_grad = prompt_grad[:, :, kv_width:].astype(jnp.bfloat16)
    return (query_grad, key_grad, value_grad, suffix_grad)
```

```python
import functools
import math

import jax
import jax.numpy as jnp
from jax import lax
from jax.experimental import pallas as pl
from jax.experimental.pallas import tpu as pltpu
from jax.sharding import PartitionSpec as P

HEAD_DIM = 128
TILE = 128
PAD = 16
FILL = -1e30
MESH = pl.DeviceIdType.MESH
F32 = jnp.float32
BF16 = jnp.bfloat16


def dot_nn(a, b):
    return lax.dot_general(a, b, (((1,), (0,)), ((), ())), preferred_element_type=F32)


def dot_nt(a, b):
    return lax.dot_general(a, b, (((1,), (1,)), ((), ())), preferred_element_type=F32)


def kernel(
    dims,
    class_ids,
    class_slot,
    pad_offset,
    suffix_pos,
    embed,
    queries,
    out_grad,
    keys,
    values,
    key_weight,
    value_weight,
    dq_out,
    dk_out,
    dv_out,
    sg_out,
    q_s,
    g_s,
    k_s,
    v_s,
    kt_s,
    wk_s,
    wv_s,
    dq_s,
    dk_s,
    dv_s,
    dk_acc,
    dv_acc,
    part,
    part_in,
    fsend,
    table,
    gsend,
    gbuf,
    w_sem,
    loc_sem,
    ex_send,
    ex_recv,
    p_send,
    p_recv,
    f_send,
    f_recv,
    g_send,
    g_recv,
    dq_loc,
    dq_send,
    dq_recv,
    dkv_loc,
    dkv_send,
    dkv_recv,
):
    dp, rows, group, own_heads = dims
    slots, suffix = embed.shape[0], embed.shape[1]
    length = 2 * rows
    width = group * HEAD_DIM
    half_kv = own_heads * HEAD_DIM
    c = lax.axis_index("ctx")
    me = lax.axis_index("dp")
    other = 1 - c
    everyone = dp * 2
    mine = me * 2 + c

    def device(index):
        return {"dp": lax.div(index, 2), "ctx": lax.rem(index, 2)}

    w_copies = [
        pltpu.make_async_copy(key_weight, wk_s, w_sem.at[0]),
        pltpu.make_async_copy(value_weight, wv_s, w_sem.at[1]),
    ]
    for copy in w_copies:
        copy.start()

    barrier = pltpu.get_barrier_semaphore()

    @pl.loop(1, everyone)
    def _(step):
        to = lax.rem(mine + step, everyone)
        pl.semaphore_signal(barrier, inc=1, device_id=device(to), device_id_type=MESH)

    def pieces(j, who):
        head = who * own_heads + j
        wide = pl.ds(pl.multiple_of(head * width, width), width)
        slim = pl.ds(pl.multiple_of(head * HEAD_DIM, HEAD_DIM), HEAD_DIM)
        at = pl.ds(pl.multiple_of(c * rows, 16), rows)
        at_kv = pl.ds(pl.multiple_of(PAD + c * rows, 16), rows)
        return [
            (queries.at[0, :, wide], q_s.at[j, at]),
            (keys.at[0, :, slim], k_s.at[j, at_kv]),
            (out_grad.at[0, :, wide], g_s.at[j, at]),
            (values.at[0, :, slim], v_s.at[j, at_kv]),
        ]

    def local_copies(j):
        return [
            pltpu.make_async_copy(src, dst, loc_sem.at[j, n])
            for n, (src, dst) in enumerate(pieces(j, c))
        ]

    def remote_copies(j):
        return [
            pltpu.make_async_remote_copy(
                src_ref=src,
                dst_ref=dst,
                send_sem=ex_send.at[j, n],
                recv_sem=ex_recv.at[j, n],
                device_id={"ctx": other},
                device_id_type=MESH,
            )
            for n, (src, dst) in enumerate(pieces(j, other))
        ]

    def incoming(j):
        at = pl.ds(pl.multiple_of(other * rows, 16), rows)
        at_kv = pl.ds(pl.multiple_of(PAD + other * rows, 16), rows)
        dsts = [q_s.at[j, at], k_s.at[j, at_kv], g_s.at[j, at], v_s.at[j, at_kv]]
        return [
            pltpu.make_async_remote_copy(
                src_ref=dst,
                dst_ref=dst,
                send_sem=ex_send.at[j, n],
                recv_sem=ex_recv.at[j, n],
                device_id={"ctx": other},
                device_id_type=MESH,
            )
            for n, dst in enumerate(dsts)
        ]

    for j in range(own_heads):
        for copy in local_copies(j):
            copy.start()

    pl.semaphore_wait(barrier, everyone - 1)

    for j in range(own_heads):
        for copy in remote_copies(j):
            copy.start()

    stacked = jnp.concatenate([embed[s].astype(F32) for s in range(slots)], axis=0).astype(BF16)
    for copy in w_copies:
        copy.wait()
    part[0] = dot_nn(stacked, wk_s[...])
    part[1] = dot_nn(stacked, wv_s[...])

    def head_columns(who):
        return pl.ds(pl.multiple_of(who * half_kv, half_kv), half_kv)

    swap = pltpu.make_async_remote_copy(
        src_ref=part.at[:, :, head_columns(other)],
        dst_ref=part_in,
        send_sem=p_send,
        recv_sem=p_recv,
        device_id={"ctx": other},
        device_id_type=MESH,
    )
    swap.start()
    picked = class_slot[class_ids[0]]
    swap.wait()
    block = slots * suffix
    fsend[0:block] = (part[0, :, head_columns(c)] + part_in[0]).astype(BF16)
    fsend[block : 2 * block] = (part[1, :, head_columns(c)] + part_in[1]).astype(BF16)
    fsend[2 * block : 2 * block + 16] = jnp.full((16, half_kv), picked, jnp.int32).astype(F32).astype(BF16)
    table[me] = fsend[...]

    def forward_copy(to, origin):
        return pltpu.make_async_remote_copy(
            src_ref=fsend,
            dst_ref=table.at[origin],
            send_sem=f_send.at[to],
            recv_sem=f_recv.at[origin],
            device_id={"dp": to},
            device_id_type=MESH,
        )

    @pl.loop(1, dp)
    def _(step):
        forward_copy(lax.rem(me + step, dp), me).start()

    @pl.loop(1, dp)
    def _(step):
        source = lax.rem(me + step, dp)
        forward_copy(source, source).wait_recv()

    found = table[lax.div(picked, slots)].astype(F32)
    which = lax.rem(picked, slots)
    zeros = jnp.zeros((PAD - suffix, half_kv), F32)
    sk = found[0:suffix]
    sv = found[block : block + suffix]
    for s in range(1, slots):
        sk = jnp.where(which == s, found[s * suffix : (s + 1) * suffix], sk)
        sv = jnp.where(which == s, found[block + s * suffix : block + (s + 1) * suffix], sv)
    sk = jnp.concatenate([sk, zeros], axis=0).astype(BF16)
    sv = jnp.concatenate([sv, zeros], axis=0).astype(BF16)
    for j in range(own_heads):
        k_s[j, 0:PAD] = sk[:, j * HEAD_DIM : (j + 1) * HEAD_DIM]
        v_s[j, 0:PAD] = sv[:, j * HEAD_DIM : (j + 1) * HEAD_DIM]

    offset = pad_offset[0]
    lanes = group * TILE
    suffix_row = lax.broadcasted_iota(jnp.int32, (PAD, lanes), 0)
    suffix_at = jnp.full((PAD, lanes), length, jnp.int32)
    for t in range(suffix):
        suffix_at = jnp.where(suffix_row == t, suffix_pos[0, t], suffix_at)
    lane_pos = lax.rem(lax.broadcasted_iota(jnp.int32, (PAD, lanes), 1), TILE)
    diag_key = lax.broadcasted_iota(jnp.int32, (TILE, lanes), 0)
    diag_query = lax.rem(lax.broadcasted_iota(jnp.int32, (TILE, lanes), 1), TILE)
    scale = HEAD_DIM ** (-0.5)
    scale_two = scale * math.log2(math.e)
    tiles = length // TILE
    per_half = tiles // 2

    def own_columns(j):
        return pl.ds(pl.multiple_of((c * own_heads + j) * width, width), width)

    def own_slim(j):
        return pl.ds(pl.multiple_of((c * own_heads + j) * HEAD_DIM, HEAD_DIM), HEAD_DIM)

    def dq_local(j, half):
        src = dq_s.at[j, pl.ds(half * rows, rows)]
        return pltpu.make_async_copy(src, dq_out.at[0, :, own_columns(j)], dq_loc.at[j])

    def dq_remote(j, half):
        return pltpu.make_async_remote_copy(
            src_ref=dq_s.at[j, pl.ds(half * rows, rows)],
            dst_ref=dq_out.at[0, :, own_columns(j)],
            send_sem=dq_send.at[j],
            recv_sem=dq_recv.at[j],
            device_id={"ctx": other},
            device_id_type=MESH,
        )

    def dkv_copies(j):
        here = pl.ds(pl.multiple_of(c * rows, 16), rows)
        there = pl.ds(pl.multiple_of(other * rows, 16), rows)
        local, remote = [], []
        for n, (stage, out) in enumerate(((dk_s, dk_out), (dv_s, dv_out))):
            dst = out.at[0, :, own_slim(j)]
            local.append(pltpu.make_async_copy(stage.at[j, here], dst, dkv_loc.at[j, n]))
            remote.append(
                pltpu.make_async_remote_copy(
                    src_ref=stage.at[j, there],
                    dst_ref=dst,
                    send_sem=dkv_send.at[j, n],
                    recv_sem=dkv_recv.at[j, n],
                    device_id={"ctx": other},
                    device_id_type=MESH,
                )
            )
        return local, remote

    def one_head(j, carry):
        for copy in local_copies(j):
            copy.wait()
        for copy in incoming(j):
            copy.wait_recv()
        kt_s[...] = k_s[j].T
        for i in reversed(range(tiles)):
            at = pl.ds(i * TILE, TILE)
            count = PAD + (i + 1) * TILE
            q4 = jnp.concatenate(
                [q_s[j, at, h * HEAD_DIM : (h + 1) * HEAD_DIM] for h in range(group)], axis=0
            )
            g4 = jnp.concatenate(
                [g_s[j, at, h * HEAD_DIM : (h + 1) * HEAD_DIM] for h in range(group)], axis=0
            )
            scores = dot_nt(k_s[j, 0:count], q4) * scale_two
            seen = [jnp.where(suffix_at <= lane_pos + i * TILE, scores[0:PAD], FILL)]
            if i > 0:
                row = lax.broadcasted_iota(jnp.int32, (i * TILE, lanes), 0)
                seen.append(jnp.where(row >= offset, scores[PAD : PAD + i * TILE], FILL))
            visible = (diag_key == diag_query) | (
                (diag_key < diag_query) & (diag_key + i * TILE >= offset)
            )
            seen.append(jnp.where(visible, scores[PAD + i * TILE :], FILL))
            scores = jnp.concatenate(seen, axis=0)
            row_max = jnp.max(scores, axis=0, keepdims=True)
            expo = jnp.exp2(scores - row_max)
            total = jnp.sum(expo, axis=0, keepdims=True)
            prob_grad = dot_nt(v_s[j, 0:count], g4)
            inverse = 1.0 / total
            delta = jnp.sum(expo * prob_grad, axis=0, keepdims=True) * inverse
            probs = expo * inverse
            score_grad = (probs * (prob_grad - delta)).astype(BF16)
            part_dv = dot_nn(probs.astype(BF16), g4)
            part_dk = dot_nn(score_grad, q4)
            if i == tiles - 1:
                dv_acc[...] = part_dv
                dk_acc[...] = part_dk
            else:
                dv_acc[0:count] += part_dv
                dk_acc[0:count] += part_dk
            dqt = dot_nn(kt_s[:, 0:count], score_grad) * scale
            for h in range(group):
                dq_s[j, at, h * HEAD_DIM : (h + 1) * HEAD_DIM] = dqt[
                    :, h * TILE : (h + 1) * TILE
                ].T.astype(BF16)
            if i % per_half == 0:
                half = i // per_half

                @pl.when(c == half)
                def _():
                    dq_local(j, half).start()

                @pl.when(c != half)
                def _():
                    dq_remote(j, half).start()

        dk_s[j] = (dk_acc[PAD:] * scale).astype(BF16)
        dv_s[j] = dv_acc[PAD:].astype(BF16)
        local, remote = dkv_copies(j)
        for copy in local + remote:
            copy.start()
        ends = jnp.concatenate([dk_acc[0:suffix] * scale, dv_acc[0:suffix]], axis=0)
        gsend[:, pl.ds(pl.multiple_of(j * HEAD_DIM, HEAD_DIM), HEAD_DIM)] = ends.astype(BF16)
        return carry

    lax.fori_loop(0, own_heads, one_head, 0)

    gbuf[mine] = gsend[...]

    def grad_copy(to, origin):
        return pltpu.make_async_remote_copy(
            src_ref=gsend,
            dst_ref=gbuf.at[origin],
            send_sem=g_send.at[to],
            recv_sem=g_recv.at[origin],
            device_id=device(to),
            device_id_type=MESH,
        )

    @pl.loop(1, everyone)
    def _(step):
        grad_copy(lax.rem(mine + step, everyone), mine).start()

    @pl.loop(1, everyone)
    def _(step):
        source = lax.rem(mine + step, everyone)
        grad_copy(source, source).wait_recv()

    def add_prompt(b, sums):
        slot_of = table[b, 2 * block : 2 * block + 16].astype(F32)
        result = []
        for s in range(slots):
            match = slot_of == (me * slots + s).astype(F32)
            for half in range(2):
                term = jnp.where(match, gbuf[b * 2 + half].astype(F32), 0.0)
                result.append(sums[s * 2 + half] + term)
        return tuple(result)

    zero = jnp.zeros((2 * suffix, half_kv), F32)
    sums = lax.fori_loop(0, dp, add_prompt, (zero,) * (2 * slots))
    projected = jnp.zeros((slots * suffix, wk_s.shape[0]), F32)
    for n, weight in enumerate((wk_s, wv_s)):
        full = jnp.concatenate(
            [
                jnp.concatenate(
                    [sums[s * 2 + half][n * suffix : (n + 1) * suffix] for half in range(2)], axis=1
                )
                for s in range(slots)
            ],
            axis=0,
        )
        high = full.astype(BF16)
        low = (full - high.astype(F32)).astype(BF16)
        both = dot_nt(jnp.concatenate([high, low], axis=0), weight[...])
        projected = projected + both[0:block] + both[block:]
    for s in range(slots):
        sg_out[s] = projected[s * suffix : (s + 1) * suffix]

    for j in range(own_heads):
        for copy in remote_copies(j):
            copy.wait_send()
        dq_local(j, 0).wait()
        dq_remote(j, 0).wait()
        local, remote = dkv_copies(j)
        for copy in local + remote:
            copy.wait()

    @pl.loop(1, dp)
    def _(step):
        forward_copy(lax.rem(me + step, dp), me).wait_send()

    @pl.loop(1, everyone)
    def _(step):
        grad_copy(lax.rem(mine + step, everyone), mine).wait_send()


def per_device(
    queries,
    keys,
    values,
    out_grad,
    key_weight,
    value_weight,
    suffix_embed,
    class_ids,
    class_slot,
    pad_offset,
    suffix_pos,
):
    dp = lax.axis_size("dp")
    rows = queries.shape[1]
    kv_width = keys.shape[2]
    group = queries.shape[2] // kv_width
    own_heads = kv_width // HEAD_DIM // 2
    slots, suffix, depth = suffix_embed.shape
    block = slots * suffix
    length = 2 * rows
    width = group * HEAD_DIM
    half_kv = own_heads * HEAD_DIM
    dma = pltpu.SemaphoreType.DMA
    smem = pl.BlockSpec(memory_space=pltpu.SMEM)
    vmem = pl.BlockSpec(memory_space=pltpu.VMEM)
    anywhere = pl.BlockSpec(memory_space=pl.ANY)
    like = lambda x, dtype: jax.ShapeDtypeStruct(x.shape, dtype)
    return pl.pallas_call(
        functools.partial(kernel, (dp, rows, group, own_heads)),
        out_shape=(
            like(queries, BF16),
            like(keys, BF16),
            like(values, BF16),
            like(suffix_embed, F32),
        ),
        in_specs=[smem] * 4 + [vmem] + [anywhere] * 6,
        out_specs=(anywhere, anywhere, anywhere, vmem),
        scratch_shapes=[
            pltpu.VMEM((own_heads, length, width), BF16),
            pltpu.VMEM((own_heads, length, width), BF16),
            pltpu.VMEM((own_heads, PAD + length, HEAD_DIM), BF16),
            pltpu.VMEM((own_heads, PAD + length, HEAD_DIM), BF16),
            pltpu.VMEM((HEAD_DIM, PAD + length), BF16),
            pltpu.VMEM((depth, kv_width), BF16),
            pltpu.VMEM((depth, kv_width), BF16),
            pltpu.VMEM((own_heads, length, width), BF16),
            pltpu.VMEM((own_heads, length, HEAD_DIM), BF16),
            pltpu.VMEM((own_heads, length, HEAD_DIM), BF16),
            pltpu.VMEM((PAD + length, HEAD_DIM), F32),
            pltpu.VMEM((PAD + length, HEAD_DIM), F32),
            pltpu.VMEM((2, block, kv_width), F32),
            pltpu.VMEM((2, block, half_kv), F32),
            pltpu.VMEM((2 * block + 16, half_kv), BF16),
            pltpu.VMEM((dp, 2 * block + 16, half_kv), BF16),
            pltpu.VMEM((2 * suffix, half_kv), BF16),
            pltpu.VMEM((dp * 2, 2 * suffix, half_kv), BF16),
            dma((2,)),
            dma((own_heads, 4)),
            dma((own_heads, 4)),
            dma((own_heads, 4)),
            dma,
            dma,
            dma((dp,)),
            dma((dp,)),
            dma((dp * 2,)),
            dma((dp * 2,)),
            dma((own_heads,)),
            dma((own_heads,)),
            dma((own_heads,)),
            dma((own_heads, 2)),
            dma((own_heads, 2)),
            dma((own_heads, 2)),
        ],
        compiler_params=pltpu.CompilerParams(
            collective_id=0, has_side_effects=True, vmem_limit_bytes=48 * 1024 * 1024
        ),
    )(
        class_ids,
        class_slot,
        pad_offset,
        suffix_pos,
        suffix_embed,
        queries,
        out_grad,
        keys,
        values,
        key_weight,
        value_weight,
    )


def solution(mesh):
    return jax.shard_map(
        per_device,
        mesh=mesh,
        in_specs=(
            P(("groups", "dp"), "ctx", None),
            P(("groups", "dp"), "ctx", None),
            P(("groups", "dp"), "ctx", None),
            P(("groups", "dp"), "ctx", None),
            P("ctx", None),
            P("ctx", None),
            P(("groups", "dp"), None, "ctx"),
            P(("groups", "dp")),
            P("groups"),
            P(("groups", "dp")),
            P(("groups", "dp"), None),
        ),
        out_specs=(
            P(("groups", "dp"), "ctx", None),
            P(("groups", "dp"), "ctx", None),
            P(("groups", "dp"), "ctx", None),
            P(("groups", "dp"), None, "ctx"),
        ),
        check_vma=False,
    )
```

```python
import functools
import math

import jax
import jax.numpy as jnp
from jax import lax
from jax.experimental import pallas as pl
from jax.experimental.pallas import tpu as pltpu
from jax.sharding import PartitionSpec as P

HEAD_DIM = 128
TILE = 128
PAD = 16
FILL = -1e30
MESH = pl.DeviceIdType.MESH
F32 = jnp.float32
BF16 = jnp.bfloat16


def dot_nn(a, b):
    return lax.dot_general(a, b, (((1,), (0,)), ((), ())), preferred_element_type=F32)


def dot_nt(a, b):
    return lax.dot_general(a, b, (((1,), (1,)), ((), ())), preferred_element_type=F32)


def kernel(
    dims,
    class_ids,
    class_slot,
    pad_offset,
    suffix_pos,
    embed,
    queries,
    out_grad,
    keys,
    values,
    key_weight,
    value_weight,
    dq_out,
    dk_out,
    dv_out,
    sg_out,
    q_s,
    g_s,
    k_s,
    v_s,
    ks_s,
    vs_s,
    kt_s,
    expo_s,
    pg_s,
    stats,
    wk_s,
    wv_s,
    dq_s,
    dq_b,
    dk_s,
    dv_s,
    dk_acc,
    dv_acc,
    part,
    part_in,
    fsend,
    table,
    gsend,
    gbuf,
    w_sem,
    loc_sem,
    ex_send,
    ex_recv,
    p_send,
    p_recv,
    f_send,
    f_recv,
    gp_send,
    gp_recv,
    g_send,
    g_recv,
    dq_loc,
    dq_send,
    dq_recv,
    dkv_loc,
    dkv_send,
    dkv_recv,
):
    dp, rows, group, own_heads = dims
    slots, suffix = embed.shape[0], embed.shape[1]
    length = 2 * rows
    width = group * HEAD_DIM
    half_kv = own_heads * HEAD_DIM
    c = lax.axis_index("ctx")
    me = lax.axis_index("dp")
    other = 1 - c
    w_copies = [
        pltpu.make_async_copy(key_weight, wk_s, w_sem.at[0]),
        pltpu.make_async_copy(value_weight, wv_s, w_sem.at[1]),
    ]
    for copy in w_copies:
        copy.start()

    barrier = pltpu.get_barrier_semaphore()

    pl.semaphore_signal(barrier, inc=1, device_id={"ctx": other}, device_id_type=MESH)

    @pl.loop(1, dp)
    def _(step):
        to = lax.rem(me + step, dp)
        pl.semaphore_signal(barrier, inc=1, device_id={"dp": to}, device_id_type=MESH)

    def pieces(j, who):
        head = who * own_heads + j
        wide = pl.ds(pl.multiple_of(head * width, width), width)
        slim = pl.ds(pl.multiple_of(head * HEAD_DIM, HEAD_DIM), HEAD_DIM)
        at = pl.ds(pl.multiple_of(c * rows, 16), rows)
        at_kv = pl.ds(pl.multiple_of(c * rows, 16), rows)
        return [
            (queries.at[0, :, wide], q_s.at[j, at]),
            (keys.at[0, :, slim], k_s.at[j, at_kv]),
            (out_grad.at[0, :, wide], g_s.at[j, at]),
            (values.at[0, :, slim], v_s.at[j, at_kv]),
        ]

    def local_copies(j):
        return [
            pltpu.make_async_copy(src, dst, loc_sem.at[j, n])
            for n, (src, dst) in enumerate(pieces(j, c))
        ]

    def remote_copies(j):
        return [
            pltpu.make_async_remote_copy(
                src_ref=src,
                dst_ref=dst,
                send_sem=ex_send.at[j, n],
                recv_sem=ex_recv.at[j, n],
                device_id={"ctx": other},
                device_id_type=MESH,
            )
            for n, (src, dst) in enumerate(pieces(j, other))
        ]

    def incoming(j):
        at = pl.ds(pl.multiple_of(other * rows, 16), rows)
        at_kv = pl.ds(pl.multiple_of(other * rows, 16), rows)
        dsts = [q_s.at[j, at], k_s.at[j, at_kv], g_s.at[j, at], v_s.at[j, at_kv]]
        return [
            pltpu.make_async_remote_copy(
                src_ref=dst,
                dst_ref=dst,
                send_sem=ex_send.at[j, n],
                recv_sem=ex_recv.at[j, n],
                device_id={"ctx": other},
                device_id_type=MESH,
            )
            for n, dst in enumerate(dsts)
        ]

    for j in range(own_heads):
        for copy in local_copies(j):
            copy.start()

    pl.semaphore_wait(barrier, dp)

    for copy in remote_copies(0):
        copy.start()

    stacked = jnp.concatenate([embed[s].astype(F32) for s in range(slots)], axis=0).astype(BF16)
    for copy in w_copies:
        copy.wait()
    part[0] = dot_nn(stacked, wk_s[...])
    part[1] = dot_nn(stacked, wv_s[...])

    def head_columns(who):
        return pl.ds(pl.multiple_of(who * half_kv, half_kv), half_kv)

    swap = pltpu.make_async_remote_copy(
        src_ref=part.at[:, :, head_columns(other)],
        dst_ref=part_in,
        send_sem=p_send,
        recv_sem=p_recv,
        device_id={"ctx": other},
        device_id_type=MESH,
    )
    swap.start()
    picked = class_slot[class_ids[0]]
    swap.wait()
    block = slots * suffix
    fsend[0:block] = (part[0, :, head_columns(c)] + part_in[0]).astype(BF16)
    fsend[block : 2 * block] = (part[1, :, head_columns(c)] + part_in[1]).astype(BF16)
    fsend[2 * block : 2 * block + 16] = jnp.full((16, half_kv), picked, jnp.int32).astype(F32).astype(BF16)
    table[me] = fsend[...]

    def forward_copy(to, origin):
        return pltpu.make_async_remote_copy(
            src_ref=fsend,
            dst_ref=table.at[origin],
            send_sem=f_send.at[to],
            recv_sem=f_recv.at[origin],
            device_id={"dp": to},
            device_id_type=MESH,
        )

    @pl.loop(1, dp)
    def _(step):
        forward_copy(lax.rem(me + step, dp), me).start()

    for j in range(1, own_heads):
        for before, copy in zip(remote_copies(j - 1), remote_copies(j)):
            before.wait_send()
            copy.start()

    offset = pad_offset[0]
    lanes = group * TILE
    suffix_row = lax.broadcasted_iota(jnp.int32, (PAD, lanes), 0)
    suffix_at = jnp.full((PAD, lanes), length, jnp.int32)
    for t in range(suffix):
        suffix_at = jnp.where(suffix_row == t, suffix_pos[0, t], suffix_at)
    lane_pos = lax.rem(lax.broadcasted_iota(jnp.int32, (PAD, lanes), 1), TILE)
    diag_key = lax.broadcasted_iota(jnp.int32, (TILE, lanes), 0)
    diag_query = lax.rem(lax.broadcasted_iota(jnp.int32, (TILE, lanes), 1), TILE)
    scale = HEAD_DIM ** (-0.5)
    scale_two = scale * math.log2(math.e)
    tiles = length // TILE
    per_half = tiles // 2

    def own_columns(j):
        return pl.ds(pl.multiple_of((c * own_heads + j) * width, width), width)

    def own_slim(j):
        return pl.ds(pl.multiple_of((c * own_heads + j) * HEAD_DIM, HEAD_DIM), HEAD_DIM)

    def dq_local(j, half):
        src = dq_b.at[j, pl.ds(half * rows, rows)]
        return pltpu.make_async_copy(src, dq_out.at[0, :, own_columns(j)], dq_loc.at[j])

    def dq_remote(j, half):
        return pltpu.make_async_remote_copy(
            src_ref=dq_b.at[j, pl.ds(half * rows, rows)],
            dst_ref=dq_out.at[0, :, own_columns(j)],
            send_sem=dq_send.at[j],
            recv_sem=dq_recv.at[j],
            device_id={"ctx": other},
            device_id_type=MESH,
        )

    def dkv_copies(j):
        here = pl.ds(pl.multiple_of(c * rows, 16), rows)
        there = pl.ds(pl.multiple_of(other * rows, 16), rows)
        local, remote = [], []
        for n, (stage, out) in enumerate(((dk_s, dk_out), (dv_s, dv_out))):
            dst = out.at[0, :, own_slim(j)]
            local.append(pltpu.make_async_copy(stage.at[j, here], dst, dkv_loc.at[j, n]))
            remote.append(
                pltpu.make_async_remote_copy(
                    src_ref=stage.at[j, there],
                    dst_ref=dst,
                    send_sem=dkv_send.at[j, n],
                    recv_sem=dkv_recv.at[j, n],
                    device_id={"ctx": other},
                    device_id_type=MESH,
                )
            )
        return local, remote

    def tile_rows(ref, j, i):
        at = pl.ds(i * TILE, TILE)
        return jnp.concatenate(
            [ref[j, at, h * HEAD_DIM : (h + 1) * HEAD_DIM] for h in range(group)], axis=0
        )

    def first_row(i):
        return i * (i + 1) // 2 * TILE

    def prompt_head(j, carry):
        for copy in local_copies(j):
            copy.wait()
        for copy in incoming(j):
            copy.wait_recv()
        for i in range(tiles):
            count = (i + 1) * TILE
            scores = dot_nt(k_s[j, 0:count], tile_rows(q_s, j, i)) * scale_two
            seen = []
            if i > 0:
                row = lax.broadcasted_iota(jnp.int32, (i * TILE, lanes), 0)
                seen.append(jnp.where(row >= offset, scores[0 : i * TILE], FILL))
            visible = (diag_key == diag_query) | (
                (diag_key < diag_query) & (diag_key + i * TILE >= offset)
            )
            seen.append(jnp.where(visible, scores[i * TILE :], FILL))
            scores = jnp.concatenate(seen, axis=0)
            row_max = jnp.max(scores, axis=0, keepdims=True)
            expo = jnp.exp2(scores - row_max)
            prob_grad = dot_nt(v_s[j, 0:count], tile_rows(g_s, j, i))
            stats[j, i, 0:1] = row_max
            stats[j, i, 1:2] = jnp.sum(expo, axis=0, keepdims=True)
            stats[j, i, 2:3] = jnp.sum(expo * prob_grad, axis=0, keepdims=True)
            expo_s[j, first_row(i) : first_row(i) + count] = expo
            pg_s[j, first_row(i) : first_row(i) + count] = prob_grad
        return carry

    lax.fori_loop(0, own_heads, prompt_head, 0)

    @pl.loop(1, dp)
    def _(step):
        source = lax.rem(me + step, dp)
        forward_copy(source, source).wait_recv()

    found = table[lax.div(picked, slots)].astype(F32)
    which = lax.rem(picked, slots)
    zeros = jnp.zeros((PAD - suffix, half_kv), F32)
    sk = found[0:suffix]
    sv = found[block : block + suffix]
    for s in range(1, slots):
        sk = jnp.where(which == s, found[s * suffix : (s + 1) * suffix], sk)
        sv = jnp.where(which == s, found[block + s * suffix : block + (s + 1) * suffix], sv)
    sk = jnp.concatenate([sk, zeros], axis=0).astype(BF16)
    sv = jnp.concatenate([sv, zeros], axis=0).astype(BF16)
    for j in range(own_heads):
        ks_s[j] = sk[:, j * HEAD_DIM : (j + 1) * HEAD_DIM]
        vs_s[j] = sv[:, j * HEAD_DIM : (j + 1) * HEAD_DIM]

    def suffix_head(j, carry):
        dk_end = jnp.zeros((PAD, HEAD_DIM), F32)
        dv_end = jnp.zeros((PAD, HEAD_DIM), F32)
        for i in range(tiles):
            q4 = tile_rows(q_s, j, i)
            g4 = tile_rows(g_s, j, i)
            scores = dot_nt(ks_s[j], q4) * scale_two
            scores = jnp.where(suffix_at <= lane_pos + i * TILE, scores, FILL)
            prompt_max = stats[j, i, 0:1]
            row_max = jnp.maximum(prompt_max, jnp.max(scores, axis=0, keepdims=True))
            rescale = jnp.exp2(prompt_max - row_max)
            expo = jnp.exp2(scores - row_max)
            prob_grad = dot_nt(vs_s[j], g4)
            total = stats[j, i, 1:2] * rescale + jnp.sum(expo, axis=0, keepdims=True)
            inverse = 1.0 / total
            delta = inverse * (
                stats[j, i, 2:3] * rescale + jnp.sum(expo * prob_grad, axis=0, keepdims=True)
            )
            stats[j, i, 3:4] = rescale * inverse
            stats[j, i, 4:5] = delta
            probs = expo * inverse
            score_grad = (probs * (prob_grad - delta)).astype(BF16)
            dv_end = dv_end + dot_nn(probs.astype(BF16), g4)
            dk_end = dk_end + dot_nn(score_grad, q4)
            dq_end = lax.dot_general(
                score_grad, ks_s[j], (((0,), (0,)), ((), ())), preferred_element_type=F32
            )
            dq_s[j, pl.ds(i * TILE, TILE)] = jnp.concatenate(
                [dq_end[h * TILE : (h + 1) * TILE] for h in range(group)], axis=1
            )
        ends = jnp.concatenate([dk_end[0:suffix] * scale, dv_end[0:suffix]], axis=0)
        gsend[c, :, pl.ds(pl.multiple_of(j * HEAD_DIM, HEAD_DIM), HEAD_DIM)] = ends.astype(BF16)
        return carry

    lax.fori_loop(0, own_heads, suffix_head, 0)

    pair = pltpu.make_async_remote_copy(
        src_ref=gsend.at[c],
        dst_ref=gsend.at[c],
        send_sem=gp_send,
        recv_sem=gp_recv,
        device_id={"ctx": other},
        device_id_type=MESH,
    )
    pair.start()

    def grad_copy(to, origin):
        return pltpu.make_async_remote_copy(
            src_ref=gsend,
            dst_ref=gbuf.at[origin],
            send_sem=g_send.at[to],
            recv_sem=g_recv.at[origin],
            device_id={"dp": to},
            device_id_type=MESH,
        )

    def prompt_grads(j, carry):
        kt_s[...] = k_s[j].T
        for i in reversed(range(tiles)):
            count = (i + 1) * TILE
            at = pl.ds(i * TILE, TILE)
            q4 = tile_rows(q_s, j, i)
            g4 = tile_rows(g_s, j, i)
            probs = expo_s[j, first_row(i) : first_row(i) + count] * stats[j, i, 3:4]
            prob_grad = pg_s[j, first_row(i) : first_row(i) + count]
            score_grad = (probs * (prob_grad - stats[j, i, 4:5])).astype(BF16)
            part_dv = dot_nn(probs.astype(BF16), g4)
            part_dk = dot_nn(score_grad, q4)
            if i == tiles - 1:
                dv_acc[...] = part_dv
                dk_acc[...] = part_dk
            else:
                dv_acc[0:count] += part_dv
                dk_acc[0:count] += part_dk
            dqt = dot_nn(kt_s[:, 0:count], score_grad)
            for h in range(group):
                columns = slice(h * HEAD_DIM, (h + 1) * HEAD_DIM)
                summed = dqt[:, h * TILE : (h + 1) * TILE].T + dq_s[j, at, columns]
                dq_b[j, at, columns] = (summed * scale).astype(BF16)
            if i % per_half == 0:
                half = i // per_half

                @pl.when(c == half)
                def _():
                    dq_local(j, half).start()

                @pl.when(c != half)
                def _():
                    dq_remote(j, half).start()

        dk_s[j] = (dk_acc[...] * scale).astype(BF16)
        dv_s[j] = dv_acc[...].astype(BF16)
        local, remote = dkv_copies(j)
        for copy in local + remote:
            copy.start()

        @pl.when(j == 0)
        def _():
            pair.wait_send()
            gpair_in.wait_recv()
            gbuf[me] = gsend[...]

            @pl.loop(1, dp)
            def _(step):
                grad_copy(lax.rem(me + step, dp), me).start()

        return carry

    gpair_in = pltpu.make_async_remote_copy(
        src_ref=gsend.at[other],
        dst_ref=gsend.at[other],
        send_sem=gp_send,
        recv_sem=gp_recv,
        device_id={"ctx": other},
        device_id_type=MESH,
    )
    lax.fori_loop(0, own_heads, prompt_grads, 0)

    @pl.loop(1, dp)
    def _(step):
        source = lax.rem(me + step, dp)
        grad_copy(source, source).wait_recv()

    def add_prompt(b, sums):
        slot_of = table[b, 2 * block : 2 * block + 16].astype(F32)
        result = []
        for s in range(slots):
            match = slot_of == (me * slots + s).astype(F32)
            for half in range(2):
                term = jnp.where(match, gbuf[b, half].astype(F32), 0.0)
                result.append(sums[s * 2 + half] + term)
        return tuple(result)

    zero = jnp.zeros((2 * suffix, half_kv), F32)
    sums = lax.fori_loop(0, dp, add_prompt, (zero,) * (2 * slots))
    projected = jnp.zeros((slots * suffix, wk_s.shape[0]), F32)
    for n, weight in enumerate((wk_s, wv_s)):
        full = jnp.concatenate(
            [
                jnp.concatenate(
                    [sums[s * 2 + half][n * suffix : (n + 1) * suffix] for half in range(2)], axis=1
                )
                for s in range(slots)
            ],
            axis=0,
        )
        high = full.astype(BF16)
        low = (full - high.astype(F32)).astype(BF16)
        both = dot_nt(jnp.concatenate([high, low], axis=0), weight[...])
        projected = projected + both[0:block] + both[block:]
    for s in range(slots):
        sg_out[s] = projected[s * suffix : (s + 1) * suffix]

    for j in range(own_heads):
        if j == own_heads - 1:
            for copy in remote_copies(j):
                copy.wait_send()
        dq_local(j, 0).wait()
        dq_remote(j, 0).wait()
        local, remote = dkv_copies(j)
        for copy in local + remote:
            copy.wait()

    @pl.loop(1, dp)
    def _(step):
        forward_copy(lax.rem(me + step, dp), me).wait_send()

    @pl.loop(1, dp)
    def _(step):
        grad_copy(lax.rem(me + step, dp), me).wait_send()


def write_out(*refs):
    count = len(refs) // 2
    sems = refs[-1]
    copies = [
        pltpu.make_async_copy(refs[n], refs[count + n], sems.at[n]) for n in range(count)
    ]
    for copy in copies:
        copy.start()
    for copy in copies:
        copy.wait()


def per_device(
    queries,
    keys,
    values,
    out_grad,
    key_weight,
    value_weight,
    suffix_embed,
    class_ids,
    class_slot,
    pad_offset,
    suffix_pos,
):
    dp = lax.axis_size("dp")
    rows = queries.shape[1]
    kv_width = keys.shape[2]
    group = queries.shape[2] // kv_width
    own_heads = kv_width // HEAD_DIM // 2
    slots, suffix, depth = suffix_embed.shape
    block = slots * suffix
    length = 2 * rows
    width = group * HEAD_DIM
    half_kv = own_heads * HEAD_DIM
    tiles = length // TILE
    pairs = tiles * (tiles + 1) // 2 * TILE
    dma = pltpu.SemaphoreType.DMA
    smem = pl.BlockSpec(memory_space=pltpu.SMEM)
    vmem = pl.BlockSpec(memory_space=pltpu.VMEM)
    anywhere = pl.BlockSpec(memory_space=pl.ANY)
    like = lambda x, dtype: jax.ShapeDtypeStruct(x.shape, dtype)
    results = pl.pallas_call(
        functools.partial(kernel, (dp, rows, group, own_heads)),
        out_shape=(
            like(queries, BF16),
            like(keys, BF16),
            like(values, BF16),
            like(suffix_embed, F32),
        ),
        in_specs=[smem] * 4 + [vmem] + [anywhere] * 6,
        out_specs=(anywhere, anywhere, anywhere, vmem),
        scratch_shapes=[
            pltpu.VMEM((own_heads, length, width), BF16),
            pltpu.VMEM((own_heads, length, width), BF16),
            pltpu.VMEM((own_heads, length, HEAD_DIM), BF16),
            pltpu.VMEM((own_heads, length, HEAD_DIM), BF16),
            pltpu.VMEM((own_heads, PAD, HEAD_DIM), BF16),
            pltpu.VMEM((own_heads, PAD, HEAD_DIM), BF16),
            pltpu.VMEM((HEAD_DIM, length), BF16),
            pltpu.VMEM((own_heads, pairs, width), F32),
            pltpu.VMEM((own_heads, pairs, width), F32),
            pltpu.VMEM((own_heads, tiles, 8, width), F32),
            pltpu.VMEM((depth, kv_width), BF16),
            pltpu.VMEM((depth, kv_width), BF16),
            pltpu.VMEM((own_heads, length, width), F32),
            pltpu.VMEM((own_heads, length, width), BF16),
            pltpu.VMEM((own_heads, length, HEAD_DIM), BF16),
            pltpu.VMEM((own_heads, length, HEAD_DIM), BF16),
            pltpu.VMEM((length, HEAD_DIM), F32),
            pltpu.VMEM((length, HEAD_DIM), F32),
            pltpu.VMEM((2, block, kv_width), F32),
            pltpu.VMEM((2, block, half_kv), F32),
            pltpu.VMEM((2 * block + 16, half_kv), BF16),
            pltpu.VMEM((dp, 2 * block + 16, half_kv), BF16),
            pltpu.VMEM((2, 2 * suffix, half_kv), BF16),
            pltpu.VMEM((dp, 2, 2 * suffix, half_kv), BF16),
            dma((2,)),
            dma((own_heads, 4)),
            dma((own_heads, 4)),
            dma((own_heads, 4)),
            dma,
            dma,
            dma((dp,)),
            dma((dp,)),
            dma,
            dma,
            dma((dp,)),
            dma((dp,)),
            dma((own_heads,)),
            dma((own_heads,)),
            dma((own_heads,)),
            dma((own_heads, 2)),
            dma((own_heads, 2)),
            dma((own_heads, 2)),
        ],
        compiler_params=pltpu.CompilerParams(
            collective_id=0, has_side_effects=True, vmem_limit_bytes=60 * 1024 * 1024
        ),
    )(
        class_ids,
        class_slot,
        pad_offset,
        suffix_pos,
        suffix_embed,
        queries,
        out_grad,
        keys,
        values,
        key_weight,
        value_weight,
    )
    return pl.pallas_call(
        write_out,
        out_shape=tuple(like(x, x.dtype) for x in results),
        in_specs=[anywhere] * 4,
        out_specs=(anywhere,) * 4,
        scratch_shapes=[dma((4,))],
    )(*results)


def solution(mesh):
    return jax.shard_map(
        per_device,
        mesh=mesh,
        in_specs=(
            P(("groups", "dp"), "ctx", None),
            P(("groups", "dp"), "ctx", None),
            P(("groups", "dp"), "ctx", None),
            P(("groups", "dp"), "ctx", None),
            P("ctx", None),
            P("ctx", None),
            P(("groups", "dp"), None, "ctx"),
            P(("groups", "dp")),
            P("groups"),
            P(("groups", "dp")),
            P(("groups", "dp"), None),
        ),
        out_specs=(
            P(("groups", "dp"), "ctx", None),
            P(("groups", "dp"), "ctx", None),
            P(("groups", "dp"), "ctx", None),
            P(("groups", "dp"), None, "ctx"),
        ),
        check_vma=False,
    )
```

```python
import functools
import math

import jax
import jax.numpy as jnp
from jax import lax
from jax.experimental import pallas as pl
from jax.experimental.pallas import tpu as pltpu
from jax.sharding import PartitionSpec as P

HEAD_DIM = 128
TILE = 128
PAD = 16
FILL = -1e30
MESH = pl.DeviceIdType.MESH
F32 = jnp.float32
BF16 = jnp.bfloat16


def dot_nn(a, b):
    return lax.dot_general(a, b, (((1,), (0,)), ((), ())), preferred_element_type=F32)


def dot_nt(a, b):
    return lax.dot_general(a, b, (((1,), (1,)), ((), ())), preferred_element_type=F32)


def kernel(
    dims,
    class_ids,
    class_slot,
    pad_offset,
    suffix_pos,
    embed_hbm,
    queries,
    out_grad,
    keys,
    values,
    key_weight,
    value_weight,
    dq_out,
    dk_out,
    dv_out,
    sg_out,
    q_s,
    g_s,
    k_s,
    v_s,
    ks_s,
    vs_s,
    kt_s,
    expo_s,
    pg_s,
    stats,
    embed,
    wk_s,
    wv_s,
    dq_s,
    dq_b,
    dk_s,
    dv_s,
    dk_acc,
    dv_acc,
    part,
    part_in,
    fsend,
    table,
    gsend,
    gbuf,
    w_sem,
    loc_sem,
    ex_send,
    ex_recv,
    p_send,
    p_recv,
    f_send,
    f_recv,
    gp_send,
    gp_recv,
    g_send,
    g_recv,
    dq_loc,
    dq_send,
    dq_recv,
    dkv_loc,
    dkv_send,
    dkv_recv,
):
    dp, rows, group, own_heads = dims
    slots, suffix = embed.shape[0], embed.shape[1]
    length = 2 * rows
    width = group * HEAD_DIM
    half_kv = own_heads * HEAD_DIM
    c = lax.axis_index("ctx")
    me = lax.axis_index("dp")
    other = 1 - c
    w_copies = [
        pltpu.make_async_copy(embed_hbm, embed, w_sem.at[2]),
        pltpu.make_async_copy(key_weight, wk_s, w_sem.at[0]),
        pltpu.make_async_copy(value_weight, wv_s, w_sem.at[1]),
    ]
    for copy in w_copies:
        copy.start()

    barrier = pltpu.get_barrier_semaphore()

    pl.semaphore_signal(barrier, inc=1, device_id={"ctx": other}, device_id_type=MESH)

    @pl.loop(1, dp)
    def _(step):
        to = lax.rem(me + step, dp)
        pl.semaphore_signal(barrier, inc=1, device_id={"dp": to}, device_id_type=MESH)

    def pieces(j, who):
        head = who * own_heads + j
        wide = pl.ds(pl.multiple_of(head * width, width), width)
        slim = pl.ds(pl.multiple_of(head * HEAD_DIM, HEAD_DIM), HEAD_DIM)
        at = pl.ds(pl.multiple_of(c * rows, 16), rows)
        at_kv = pl.ds(pl.multiple_of(c * rows, 16), rows)
        return [
            (queries.at[0, :, wide], q_s.at[j, at]),
            (keys.at[0, :, slim], k_s.at[j, at_kv]),
            (out_grad.at[0, :, wide], g_s.at[j, at]),
            (values.at[0, :, slim], v_s.at[j, at_kv]),
        ]

    def local_copies(j):
        return [
            pltpu.make_async_copy(src, dst, loc_sem.at[j, n])
            for n, (src, dst) in enumerate(pieces(j, c))
        ]

    def remote_copies(j):
        return [
            pltpu.make_async_remote_copy(
                src_ref=src,
                dst_ref=dst,
                send_sem=ex_send.at[j, n],
                recv_sem=ex_recv.at[j, n],
                device_id={"ctx": other},
                device_id_type=MESH,
            )
            for n, (src, dst) in enumerate(pieces(j, other))
        ]

    def incoming(j):
        at = pl.ds(pl.multiple_of(other * rows, 16), rows)
        at_kv = pl.ds(pl.multiple_of(other * rows, 16), rows)
        dsts = [q_s.at[j, at], k_s.at[j, at_kv], g_s.at[j, at], v_s.at[j, at_kv]]
        return [
            pltpu.make_async_remote_copy(
                src_ref=dst,
                dst_ref=dst,
                send_sem=ex_send.at[j, n],
                recv_sem=ex_recv.at[j, n],
                device_id={"ctx": other},
                device_id_type=MESH,
            )
            for n, dst in enumerate(dsts)
        ]

    for j in range(own_heads):
        for copy in local_copies(j):
            copy.start()

    pl.semaphore_wait(barrier, dp)

    for copy in remote_copies(0):
        copy.start()

    for copy in w_copies:
        copy.wait()
    stacked = jnp.concatenate([embed[s].astype(F32) for s in range(slots)], axis=0).astype(BF16)
    part[0] = dot_nn(stacked, wk_s[...])
    part[1] = dot_nn(stacked, wv_s[...])

    def head_columns(who):
        return pl.ds(pl.multiple_of(who * half_kv, half_kv), half_kv)

    swap = pltpu.make_async_remote_copy(
        src_ref=part.at[:, :, head_columns(other)],
        dst_ref=part_in,
        send_sem=p_send,
        recv_sem=p_recv,
        device_id={"ctx": other},
        device_id_type=MESH,
    )
    swap.start()
    picked = class_slot[class_ids[0]]
    swap.wait()
    block = slots * suffix
    fsend[0:block] = (part[0, :, head_columns(c)] + part_in[0]).astype(BF16)
    fsend[block : 2 * block] = (part[1, :, head_columns(c)] + part_in[1]).astype(BF16)
    fsend[2 * block : 2 * block + 16] = jnp.full((16, half_kv), picked, jnp.int32).astype(F32).astype(BF16)
    table[me] = fsend[...]

    def forward_copy(to, origin):
        return pltpu.make_async_remote_copy(
            src_ref=fsend,
            dst_ref=table.at[origin],
            send_sem=f_send.at[to],
            recv_sem=f_recv.at[origin],
            device_id={"dp": to},
            device_id_type=MESH,
        )

    @pl.loop(1, dp)
    def _(step):
        forward_copy(lax.rem(me + step, dp), me).start()

    for j in range(1, own_heads):
        for before, copy in zip(remote_copies(j - 1), remote_copies(j)):
            before.wait_send()
            copy.start()

    offset = pad_offset[0]
    lanes = group * TILE
    suffix_row = lax.broadcasted_iota(jnp.int32, (PAD, lanes), 0)
    suffix_at = jnp.full((PAD, lanes), length, jnp.int32)
    for t in range(suffix):
        suffix_at = jnp.where(suffix_row == t, suffix_pos[0, t], suffix_at)
    lane_pos = lax.rem(lax.broadcasted_iota(jnp.int32, (PAD, lanes), 1), TILE)
    diag_key = lax.broadcasted_iota(jnp.int32, (TILE, lanes), 0)
    diag_query = lax.rem(lax.broadcasted_iota(jnp.int32, (TILE, lanes), 1), TILE)
    scale = HEAD_DIM ** (-0.5)
    scale_two = scale * math.log2(math.e)
    tiles = length // TILE
    per_half = tiles // 2

    def own_columns(j):
        return pl.ds(pl.multiple_of((c * own_heads + j) * width, width), width)

    def own_slim(j):
        return pl.ds(pl.multiple_of((c * own_heads + j) * HEAD_DIM, HEAD_DIM), HEAD_DIM)

    def dq_local(j, half):
        src = dq_b.at[j, pl.ds(half * rows, rows)]
        return pltpu.make_async_copy(src, dq_out.at[0, :, own_columns(j)], dq_loc.at[j])

    def dq_remote(j, half):
        return pltpu.make_async_remote_copy(
            src_ref=dq_b.at[j, pl.ds(half * rows, rows)],
            dst_ref=dq_out.at[0, :, own_columns(j)],
            send_sem=dq_send.at[j],
            recv_sem=dq_recv.at[j],
            device_id={"ctx": other},
            device_id_type=MESH,
        )

    def dkv_copies(j):
        here = pl.ds(pl.multiple_of(c * rows, 16), rows)
        there = pl.ds(pl.multiple_of(other * rows, 16), rows)
        local, remote = [], []
        for n, (stage, out) in enumerate(((dk_s, dk_out), (dv_s, dv_out))):
            dst = out.at[0, :, own_slim(j)]
            local.append(pltpu.make_async_copy(stage.at[j, here], dst, dkv_loc.at[j, n]))
            remote.append(
                pltpu.make_async_remote_copy(
                    src_ref=stage.at[j, there],
                    dst_ref=dst,
                    send_sem=dkv_send.at[j, n],
                    recv_sem=dkv_recv.at[j, n],
                    device_id={"ctx": other},
                    device_id_type=MESH,
                )
            )
        return local, remote

    def tile_rows(ref, j, i):
        at = pl.ds(i * TILE, TILE)
        return jnp.concatenate(
            [ref[j, at, h * HEAD_DIM : (h + 1) * HEAD_DIM] for h in range(group)], axis=0
        )

    def first_row(i):
        return i * (i + 1) // 2 * TILE

    def prompt_head(j, carry):
        for copy in local_copies(j):
            copy.wait()
        for copy in incoming(j):
            copy.wait_recv()
        for i in range(tiles):
            count = (i + 1) * TILE
            scores = dot_nt(k_s[j, 0:count], tile_rows(q_s, j, i)) * scale_two
            seen = []
            if i > 0:
                row = lax.broadcasted_iota(jnp.int32, (i * TILE, lanes), 0)
                seen.append(jnp.where(row >= offset, scores[0 : i * TILE], FILL))
            visible = (diag_key == diag_query) | (
                (diag_key < diag_query) & (diag_key + i * TILE >= offset)
            )
            seen.append(jnp.where(visible, scores[i * TILE :], FILL))
            scores = jnp.concatenate(seen, axis=0)
            row_max = jnp.max(scores, axis=0, keepdims=True)
            expo = jnp.exp2(scores - row_max)
            prob_grad = dot_nt(v_s[j, 0:count], tile_rows(g_s, j, i))
            stats[j, i, 0:1] = row_max
            stats[j, i, 1:2] = jnp.sum(expo, axis=0, keepdims=True)
            stats[j, i, 2:3] = jnp.sum(expo * prob_grad, axis=0, keepdims=True)
            expo_s[j, first_row(i) : first_row(i) + count] = expo
            pg_s[j, first_row(i) : first_row(i) + count] = prob_grad
        return carry

    lax.fori_loop(0, own_heads, prompt_head, 0)

    @pl.loop(1, dp)
    def _(step):
        source = lax.rem(me + step, dp)
        forward_copy(source, source).wait_recv()

    found = table[lax.div(picked, slots)].astype(F32)
    which = lax.rem(picked, slots)
    zeros = jnp.zeros((PAD - suffix, half_kv), F32)
    sk = found[0:suffix]
    sv = found[block : block + suffix]
    for s in range(1, slots):
        sk = jnp.where(which == s, found[s * suffix : (s + 1) * suffix], sk)
        sv = jnp.where(which == s, found[block + s * suffix : block + (s + 1) * suffix], sv)
    sk = jnp.concatenate([sk, zeros], axis=0).astype(BF16)
    sv = jnp.concatenate([sv, zeros], axis=0).astype(BF16)
    for j in range(own_heads):
        ks_s[j] = sk[:, j * HEAD_DIM : (j + 1) * HEAD_DIM]
        vs_s[j] = sv[:, j * HEAD_DIM : (j + 1) * HEAD_DIM]

    def suffix_head(j, carry):
        dk_end = jnp.zeros((PAD, HEAD_DIM), F32)
        dv_end = jnp.zeros((PAD, HEAD_DIM), F32)
        for i in range(tiles):
            q4 = tile_rows(q_s, j, i)
            g4 = tile_rows(g_s, j, i)
            scores = dot_nt(ks_s[j], q4) * scale_two
            scores = jnp.where(suffix_at <= lane_pos + i * TILE, scores, FILL)
            prompt_max = stats[j, i, 0:1]
            row_max = jnp.maximum(prompt_max, jnp.max(scores, axis=0, keepdims=True))
            rescale = jnp.exp2(prompt_max - row_max)
            expo = jnp.exp2(scores - row_max)
            prob_grad = dot_nt(vs_s[j], g4)
            total = stats[j, i, 1:2] * rescale + jnp.sum(expo, axis=0, keepdims=True)
            inverse = 1.0 / total
            delta = inverse * (
                stats[j, i, 2:3] * rescale + jnp.sum(expo * prob_grad, axis=0, keepdims=True)
            )
            stats[j, i, 3:4] = rescale * inverse
            stats[j, i, 4:5] = delta
            probs = expo * inverse
            score_grad = (probs * (prob_grad - delta)).astype(BF16)
            dv_end = dv_end + dot_nn(probs.astype(BF16), g4)
            dk_end = dk_end + dot_nn(score_grad, q4)
            dq_end = lax.dot_general(
                score_grad, ks_s[j], (((0,), (0,)), ((), ())), preferred_element_type=F32
            )
            dq_s[j, pl.ds(i * TILE, TILE)] = jnp.concatenate(
                [dq_end[h * TILE : (h + 1) * TILE] for h in range(group)], axis=1
            )
        ends = jnp.concatenate([dk_end[0:suffix] * scale, dv_end[0:suffix]], axis=0)
        gsend[c, :, pl.ds(pl.multiple_of(j * HEAD_DIM, HEAD_DIM), HEAD_DIM)] = ends.astype(BF16)
        return carry

    lax.fori_loop(0, own_heads, suffix_head, 0)

    pair = pltpu.make_async_remote_copy(
        src_ref=gsend.at[c],
        dst_ref=gsend.at[c],
        send_sem=gp_send,
        recv_sem=gp_recv,
        device_id={"ctx": other},
        device_id_type=MESH,
    )
    pair.start()

    def grad_copy(to, origin):
        return pltpu.make_async_remote_copy(
            src_ref=gsend,
            dst_ref=gbuf.at[origin],
            send_sem=g_send.at[to],
            recv_sem=g_recv.at[origin],
            device_id={"dp": to},
            device_id_type=MESH,
        )

    def prompt_grads(j, carry):
        kt_s[...] = k_s[j].T
        for i in reversed(range(tiles)):
            count = (i + 1) * TILE
            at = pl.ds(i * TILE, TILE)
            q4 = tile_rows(q_s, j, i)
            g4 = tile_rows(g_s, j, i)
            probs = expo_s[j, first_row(i) : first_row(i) + count] * stats[j, i, 3:4]
            prob_grad = pg_s[j, first_row(i) : first_row(i) + count]
            score_grad = (probs * (prob_grad - stats[j, i, 4:5])).astype(BF16)
            part_dv = dot_nn(probs.astype(BF16), g4)
            part_dk = dot_nn(score_grad, q4)
            if i == tiles - 1:
                dv_acc[...] = part_dv
                dk_acc[...] = part_dk
            else:
                dv_acc[0:count] += part_dv
                dk_acc[0:count] += part_dk
            dqt = dot_nn(kt_s[:, 0:count], score_grad)
            for h in range(group):
                columns = slice(h * HEAD_DIM, (h + 1) * HEAD_DIM)
                summed = dqt[:, h * TILE : (h + 1) * TILE].T + dq_s[j, at, columns]
                dq_b[j, at, columns] = (summed * scale).astype(BF16)
            if i % per_half == 0:
                half = i // per_half

                @pl.when(c == half)
                def _():
                    dq_local(j, half).start()

                @pl.when(c != half)
                def _():
                    dq_remote(j, half).start()

        dk_s[j] = (dk_acc[...] * scale).astype(BF16)
        dv_s[j] = dv_acc[...].astype(BF16)
        local, remote = dkv_copies(j)
        for copy in local + remote:
            copy.start()

        @pl.when(j == 0)
        def _():
            pair.wait_send()
            gpair_in.wait_recv()
            gbuf[me] = gsend[...]

            @pl.loop(1, dp)
            def _(step):
                grad_copy(lax.rem(me + step, dp), me).start()

        return carry

    gpair_in = pltpu.make_async_remote_copy(
        src_ref=gsend.at[other],
        dst_ref=gsend.at[other],
        send_sem=gp_send,
        recv_sem=gp_recv,
        device_id={"ctx": other},
        device_id_type=MESH,
    )
    lax.fori_loop(0, own_heads, prompt_grads, 0)

    @pl.loop(1, dp)
    def _(step):
        source = lax.rem(me + step, dp)
        grad_copy(source, source).wait_recv()

    def add_prompt(b, sums):
        slot_of = table[b, 2 * block : 2 * block + 16].astype(F32)
        result = []
        for s in range(slots):
            match = slot_of == (me * slots + s).astype(F32)
            for half in range(2):
                term = jnp.where(match, gbuf[b, half].astype(F32), 0.0)
                result.append(sums[s * 2 + half] + term)
        return tuple(result)

    zero = jnp.zeros((2 * suffix, half_kv), F32)
    sums = lax.fori_loop(0, dp, add_prompt, (zero,) * (2 * slots))
    projected = jnp.zeros((slots * suffix, wk_s.shape[0]), F32)
    for n, weight in enumerate((wk_s, wv_s)):
        full = jnp.concatenate(
            [
                jnp.concatenate(
                    [sums[s * 2 + half][n * suffix : (n + 1) * suffix] for half in range(2)], axis=1
                )
                for s in range(slots)
            ],
            axis=0,
        )
        high = full.astype(BF16)
        low = (full - high.astype(F32)).astype(BF16)
        both = dot_nt(jnp.concatenate([high, low], axis=0), weight[...])
        projected = projected + both[0:block] + both[block:]
    for s in range(slots):
        sg_out[s] = projected[s * suffix : (s + 1) * suffix]

    for j in range(own_heads):
        if j == own_heads - 1:
            for copy in remote_copies(j):
                copy.wait_send()
        dq_local(j, 0).wait()
        dq_remote(j, 0).wait()
        local, remote = dkv_copies(j)
        for copy in local + remote:
            copy.wait()

    @pl.loop(1, dp)
    def _(step):
        forward_copy(lax.rem(me + step, dp), me).wait_send()

    @pl.loop(1, dp)
    def _(step):
        grad_copy(lax.rem(me + step, dp), me).wait_send()


def write_out(*refs):
    count = (len(refs) - 2) // 3
    sources, results, stages = refs[:count], refs[count : 2 * count], refs[2 * count : 3 * count]
    read_sem, write_sem = refs[-2:]
    reads, writes = [], []
    for n in range(count):
        rows = sources[n].shape[1]
        step = TILE if rows % TILE == 0 else rows
        for at in range(rows // step):
            part = pl.ds(at * step, step)
            stage = stages[n].at[:, part]
            reads.append(pltpu.make_async_copy(sources[n].at[:, part], stage, read_sem.at[n, at]))
            writes.append(pltpu.make_async_copy(stage, results[n].at[:, part], write_sem.at[n, at]))
    for copy in reads:
        copy.start()
    for before, copy in zip(reads, writes):
        before.wait()
        copy.start()
    for copy in writes:
        copy.wait()


def per_device(
    queries,
    keys,
    values,
    out_grad,
    key_weight,
    value_weight,
    suffix_embed,
    class_ids,
    class_slot,
    pad_offset,
    suffix_pos,
):
    dp = lax.axis_size("dp")
    rows = queries.shape[1]
    kv_width = keys.shape[2]
    group = queries.shape[2] // kv_width
    own_heads = kv_width // HEAD_DIM // 2
    slots, suffix, depth = suffix_embed.shape
    block = slots * suffix
    length = 2 * rows
    width = group * HEAD_DIM
    half_kv = own_heads * HEAD_DIM
    tiles = length // TILE
    pairs = tiles * (tiles + 1) // 2 * TILE
    dma = pltpu.SemaphoreType.DMA
    smem = pl.BlockSpec(memory_space=pltpu.SMEM)
    vmem = pl.BlockSpec(memory_space=pltpu.VMEM)
    anywhere = pl.BlockSpec(memory_space=pl.ANY)
    like = lambda x, dtype: jax.ShapeDtypeStruct(x.shape, dtype)
    results = pl.pallas_call(
        functools.partial(kernel, (dp, rows, group, own_heads)),
        out_shape=(
            like(queries, BF16),
            like(keys, BF16),
            like(values, BF16),
            like(suffix_embed, F32),
        ),
        in_specs=[smem] * 4 + [anywhere] * 7,
        out_specs=(anywhere, anywhere, anywhere, vmem),
        scratch_shapes=[
            pltpu.VMEM((own_heads, length, width), BF16),
            pltpu.VMEM((own_heads, length, width), BF16),
            pltpu.VMEM((own_heads, length, HEAD_DIM), BF16),
            pltpu.VMEM((own_heads, length, HEAD_DIM), BF16),
            pltpu.VMEM((own_heads, PAD, HEAD_DIM), BF16),
            pltpu.VMEM((own_heads, PAD, HEAD_DIM), BF16),
            pltpu.VMEM((HEAD_DIM, length), BF16),
            pltpu.VMEM((own_heads, pairs, width), F32),
            pltpu.VMEM((own_heads, pairs, width), F32),
            pltpu.VMEM((own_heads, tiles, 8, width), F32),
            pltpu.VMEM((slots, suffix, depth), BF16),
            pltpu.VMEM((depth, kv_width), BF16),
            pltpu.VMEM((depth, kv_width), BF16),
            pltpu.VMEM((own_heads, length, width), F32),
            pltpu.VMEM((own_heads, length, width), BF16),
            pltpu.VMEM((own_heads, length, HEAD_DIM), BF16),
            pltpu.VMEM((own_heads, length, HEAD_DIM), BF16),
            pltpu.VMEM((length, HEAD_DIM), F32),
            pltpu.VMEM((length, HEAD_DIM), F32),
            pltpu.VMEM((2, block, kv_width), F32),
            pltpu.VMEM((2, block, half_kv), F32),
            pltpu.VMEM((2 * block + 16, half_kv), BF16),
            pltpu.VMEM((dp, 2 * block + 16, half_kv), BF16),
            pltpu.VMEM((2, 2 * suffix, half_kv), BF16),
            pltpu.VMEM((dp, 2, 2 * suffix, half_kv), BF16),
            dma((3,)),
            dma((own_heads, 4)),
            dma((own_heads, 4)),
            dma((own_heads, 4)),
            dma,
            dma,
            dma((dp,)),
            dma((dp,)),
            dma,
            dma,
            dma((dp,)),
            dma((dp,)),
            dma((own_heads,)),
            dma((own_heads,)),
            dma((own_heads,)),
            dma((own_heads, 2)),
            dma((own_heads, 2)),
            dma((own_heads, 2)),
        ],
        compiler_params=pltpu.CompilerParams(
            collective_id=0, has_side_effects=True, vmem_limit_bytes=60 * 1024 * 1024
        ),
    )(
        class_ids,
        class_slot,
        pad_offset,
        suffix_pos,
        suffix_embed,
        queries,
        out_grad,
        keys,
        values,
        key_weight,
        value_weight,
    )
    chunks = max(1, rows // TILE)
    return pl.pallas_call(
        write_out,
        out_shape=tuple(like(x, x.dtype) for x in results),
        in_specs=[anywhere] * 4,
        out_specs=(anywhere,) * 4,
        scratch_shapes=[pltpu.VMEM(x.shape, x.dtype) for x in results] + [dma((4, chunks)), dma((4, chunks))],
    )(*results)


def solution(mesh):
    return jax.shard_map(
        per_device,
        mesh=mesh,
        in_specs=(
            P(("groups", "dp"), "ctx", None),
            P(("groups", "dp"), "ctx", None),
            P(("groups", "dp"), "ctx", None),
            P(("groups", "dp"), "ctx", None),
            P("ctx", None),
            P("ctx", None),
            P(("groups", "dp"), None, "ctx"),
            P(("groups", "dp")),
            P("groups"),
            P(("groups", "dp")),
            P(("groups", "dp"), None),
        ),
        out_specs=(
            P(("groups", "dp"), "ctx", None),
            P(("groups", "dp"), "ctx", None),
            P(("groups", "dp"), "ctx", None),
            P(("groups", "dp"), None, "ctx"),
        ),
        check_vma=False,
    )
```
